512 devices in a mesh: outer: 8 (over x, y_hi), rep: 4 (over y_lo), shard: 16 (over z, core).
Axes of the slice: x: 4, y: 8 (y_hi: 2, y_lo: 4; y = y_hi * 4 + y_lo), z: 8, core: 2. Of those that a mesh axis runs over, the one named last changes fastest.
Arguments:
- momentum: float32 [8, 4, 1024, 8192], P('outer', 'rep', 'shard'), may hold values from -6 to 6
Outputs:
- new_momentum: float32 [8, 4, 1024, 8192], P('outer', 'rep', 'shard')
- update: bfloat16 [8, 1024, 8192], P('outer', 'shard')
The draws below stay inside these ranges and needn't reach their ends.
All inputs are finite; a program needn't handle non-finite values.
Results may differ from the reference program's by a relative error of at most 0.001.
Values sent between devices are 32-bit elements; how exact they have to be, the bound alone decides.
A program may use at most 64 MiB of HBM per device.

```python
import jax
import jax.numpy as jnp
from jax import lax

D = 8192
TILE = 64
KEEP = 16
ROWS = 1024
N_OUTER = 8
N_REP = 4


def block_levels(stream_key, dims, shards, low, high):
    def one(dim, shards_of):
        draws = jax.random.uniform(jax.random.fold_in(jax.random.fold_in(stream_key, 6), dim), (shards_of,), jnp.float32, low / len(shards), high / len(shards))
        return jnp.repeat(jnp.exp(draws), dims[dim] // shards_of).reshape((-1,) + (1,) * (len(dims) - dim - 1))

    factor_of = one(*shards[0])
    for cut in shards[1:]:
        factor_of = factor_of * one(*cut)
    return factor_of


def bell_draw(key, extent, width, most, shards=(), dtype=jnp.bfloat16):
    array = jax.random.normal(key, extent, jnp.float32) * width
    if len(shards) > 0:
        array = block_levels(key, extent, shards, -0.22, 0.18) * array
    return jnp.clip(array, min=-most, max=most).astype(dtype)


def setup_inputs(seed: int = 0) -> dict:
    key_list = jax.random.split(jax.random.key(seed), 2)
    return {
        "momentum": bell_draw(key_list[0], (N_OUTER, N_REP, ROWS, D), 1.0, 6.0, ((0, 8), (1, 4), (2, 16)), jnp.float32),
    }


def low_basis():
    index = jnp.arange(TILE).astype(jnp.float32)
    freq = jnp.arange(KEEP).astype(jnp.float32)
    angles = jnp.pi * (2.0 * index[None, :] + 1.0) * freq[:, None] / (2.0 * TILE)
    scales = jnp.where(freq == 0.0, jnp.sqrt(1.0 / TILE), jnp.sqrt(2.0 / TILE)).astype(jnp.float32)
    return (scales[:, None] * jnp.cos(angles)).astype(jnp.float32)

def encode(block, basis):
    rows, cols = block.shape
    tiled = block.reshape(rows // TILE, TILE, cols)
    left = jnp.einsum('kr,trd->tkd', basis, tiled, precision=lax.Precision.HIGHEST)
    left = left.reshape(rows // TILE, KEEP, cols // TILE, TILE)
    return jnp.einsum('tknc,lc->tknl', left, basis, precision=lax.Precision.HIGHEST)

def decode(coeffs, basis):
    tiles, keep, ncol, keep2 = coeffs.shape
    right = jnp.einsum('tknl,lc->tknc', coeffs, basis, precision=lax.Precision.HIGHEST)
    right = right.reshape(tiles, KEEP, ncol * TILE)
    full = jnp.einsum('kr,tkd->trd', basis, right, precision=lax.Precision.HIGHEST)
    return full.reshape(tiles * TILE, ncol * TILE)

def reference(momentum):
    basis = low_basis()

    def pod_work(pod_momentum):
        coeffs = jax.vmap(lambda b: encode(b, basis))(pod_momentum)
        fresh = pod_momentum - jax.vmap(lambda c: decode(c, basis))(coeffs)
        return (lax.optimization_barrier(jnp.sum(coeffs, axis=0)), fresh)
    pod_sum, new_momentum = lax.map(pod_work, momentum)
    mixed = 0.5 * pod_sum + 0.25 * (jnp.roll(pod_sum, 1, axis=0) + jnp.roll(pod_sum, -1, axis=0))
    update = lax.map(lambda c: decode(c, basis), mixed).astype(jnp.bfloat16)
    return (new_momentum, update)
```

```python
import functools

import jax
import jax.numpy as jnp
import ml_dtypes
import numpy as np
from jax import lax
from jax.experimental import pallas as pl
from jax.experimental.pallas import tpu as pltpu
from jax.sharding import PartitionSpec as P

TILE = 64
KEEP = 16
RING = 8
POD = 4
GROUP = 8
MESH = pl.DeviceIdType.MESH
BF16 = jnp.bfloat16
F32 = jnp.float32


def low_basis():
    index = np.arange(TILE)
    freq = np.arange(KEEP)
    angles = np.pi * (2.0 * index[None, :] + 1.0) * freq[:, None] / (2.0 * TILE)
    scales = np.where(freq == 0, np.sqrt(1.0 / TILE), np.sqrt(2.0 / TILE))
    return (scales[:, None] * np.cos(angles)).astype(np.float32)


def halves(array):
    high = array.astype(ml_dtypes.bfloat16)
    low = (array - high.astype(np.float32)).astype(ml_dtypes.bfloat16)
    return high, low


def tables():
    basis = low_basis()
    high, low = (half.astype(np.float32) for half in halves(basis))
    out = np.zeros((208, 256), np.float32)
    out[:128, :128] = np.tile(basis, (GROUP, 2))
    out[:128, 128:] = np.tile(basis.T, (2, GROUP))
    out[128:144, :192] = np.concatenate([high, low, high], axis=1)
    out[144:, :48] = np.concatenate([high.T, high.T, low.T], axis=1)
    return out


def set_up(table, enc_cols, enc_rows, dec_cols, dec_rows):
    for place in range(4):
        lanes = pl.ds(place * 128, 128)
        row = lax.broadcasted_iota(jnp.int32, (128, 128), 0)
        col = lax.broadcasted_iota(jnp.int32, (128, 128), 1)
        high, low = split(jnp.where(row // KEEP == 2 * place + col // TILE, table[:128, :128], 0.0))
        dec_cols[:128, lanes] = high
        dec_cols[128:256, lanes] = high
        dec_cols[256:, lanes] = low
        high, low = split(jnp.where(col // KEEP == 2 * place + row // TILE, table[:128, 128:], 0.0))
        enc_cols[lanes, :128] = high
        enc_cols[lanes, 128:] = low
    enc_rows[...] = table[128:144, :192].astype(BF16)
    dec_rows[...] = table[144:, :48].astype(BF16)


def split(value):
    high = value.astype(BF16)
    low = (value - high.astype(F32)).astype(BF16)
    return high, low


def dot(a, b):
    return jnp.dot(a, b, preferred_element_type=F32)


def encode(x, enc_cols, enc_rows):
    groups = x.shape[1] // (GROUP * TILE)
    tall = jnp.concatenate([x[:, g * 512:(g + 1) * 512] for g in range(groups)], axis=0)
    high, low = split(tall)
    both = dot(high, enc_cols[...])
    right = both[:, :128] + both[:, 128:] + dot(low, enc_cols[:, :128])
    right = jnp.concatenate([right[g * TILE:(g + 1) * TILE] for g in range(groups)], axis=1)
    high, low = split(right)
    return dot(enc_rows[...], jnp.concatenate([high, high, low], axis=0))


def decode(c, dec_cols, dec_rows):
    groups = c.shape[1] // 128
    tall = jnp.concatenate([c[:, g * 128:(g + 1) * 128] for g in range(groups)], axis=0)
    high, low = split(tall)
    right = dot(jnp.concatenate([high, low, high], axis=1), dec_cols[...])
    right = jnp.concatenate([right[g * KEEP:(g + 1) * KEEP] for g in range(groups)], axis=1)
    high, low = split(right)
    return dot(dec_rows[...], jnp.concatenate([high, low, high], axis=0))


def kernel(x_hbm, table_hbm, fresh, update,
           x, table, enc_cols, enc_rows, dec_cols, dec_rows, coeffs, parts, sums, around, mixed, got,
           x_sem, table_sem, rs_send, rs_recv, x_send, x_recv, ag_send, ag_recv):
    outer, rep = lax.axis_index("outer"), lax.axis_index("rep")
    columns = lax.axis_size("outer") // 2
    column, side = outer // 2, outer % 2
    me = side * POD + rep
    width = x.shape[1] // RING
    kept = coeffs.shape[2]

    def ring(place):
        return {"outer": column * 2 + place // POD, "rep": place % POD}

    def beside(step):
        return {"outer": lax.rem(column + step + columns, columns) * 2 + side}

    def off(step):
        half = (step + 1) // 2
        return 4 + half * (1 - 2 * (step % 2))

    def chunk(place):
        return pl.ds(pl.multiple_of(place * width, width), width)

    def load(place):
        return pltpu.make_async_copy(x_hbm.at[0, 0, :, chunk(place)], x.at[:, chunk(place)], x_sem.at[place])

    def place_at(step):
        return lax.rem(me + off(step), RING)

    table_copy = pltpu.make_async_copy(table_hbm, table, table_sem)
    table_copy.start()
    for step in range(RING):
        load(place_at(step)).start()

    barrier = pltpu.get_barrier_semaphore()
    for step in range(1, RING):
        pl.semaphore_signal(barrier, inc=1, device_id=ring(lax.rem(me + step, RING)), device_id_type=MESH)
    for step in (1, -1):
        pl.semaphore_signal(barrier, inc=1, device_id=beside(step), device_id_type=MESH)

    def encode_at(place):
        load(place).wait()
        coeffs[place] = encode(x[:, chunk(place)], enc_cols, enc_rows)

    def share(place):
        return pltpu.make_async_remote_copy(
            src_ref=coeffs.at[place], dst_ref=parts.at[me], send_sem=rs_send.at[place], recv_sem=rs_recv.at[me],
            device_id=ring(place), device_id_type=MESH)

    def arrived(place):
        return pltpu.make_async_remote_copy(
            src_ref=coeffs.at[place], dst_ref=parts.at[place], send_sem=rs_send.at[place], recv_sem=rs_recv.at[place],
            device_id=ring(place), device_id_type=MESH)

    table_copy.wait()
    set_up(table, enc_cols, enc_rows, dec_cols, dec_rows)
    encode_at(place_at(0))
    pl.semaphore_wait(barrier, RING + 1)
    share(place_at(0)).start()

    @pl.loop(1, RING - 1)
    def _(step):
        place = place_at(step)
        encode_at(place)
        share(place).start()

    encode_at(me)
    parts[me] = coeffs[me]

    @pl.loop(0, RING)
    def _(place):
        fresh[0, 0, :, chunk(place)] = x[:, chunk(place)] - decode(coeffs[place], dec_cols, dec_rows)

    @pl.loop(1, RING)
    def _(step):
        arrived(lax.rem(me + step, RING)).wait_recv()

    sums[0] = parts[0] + parts[1] + parts[2] + parts[3]
    sums[1] = parts[4] + parts[5] + parts[6] + parts[7]
    to_next = pltpu.make_async_remote_copy(
        src_ref=sums.at[1], dst_ref=around.at[0], send_sem=x_send.at[0], recv_sem=x_recv.at[0],
        device_id=beside(1), device_id_type=MESH)
    to_prev = pltpu.make_async_remote_copy(
        src_ref=sums.at[0], dst_ref=around.at[1], send_sem=x_send.at[1], recv_sem=x_recv.at[1],
        device_id=beside(-1), device_id_type=MESH)
    to_next.start()
    to_prev.start()
    first = 0.5 * sums[0] + 0.25 * sums[1]
    second = 0.5 * sums[1] + 0.25 * sums[0]
    to_next.wait_recv()
    mixed[0] = first + 0.25 * around[0]
    to_prev.wait_recv()
    mixed[1] = second + 0.25 * around[1]

    def spread(place):
        return pltpu.make_async_remote_copy(
            src_ref=mixed.at[place // POD], dst_ref=got.at[me], send_sem=ag_send.at[place], recv_sem=ag_recv.at[me],
            device_id=ring(place), device_id_type=MESH)

    def landed(place):
        return pltpu.make_async_remote_copy(
            src_ref=mixed.at[0], dst_ref=got.at[place], send_sem=ag_send.at[place], recv_sem=ag_recv.at[place],
            device_id=ring(place), device_id_type=MESH)

    @pl.loop(0, RING - 1)
    def _(step):
        spread(place_at(step)).start()

    got[me] = mixed[side]

    def decode_at(place):
        update[0, :, chunk(place)] = decode(got[place], dec_cols, dec_rows).astype(BF16)

    decode_at(me)

    @pl.loop(1, RING)
    def _(step):
        place = place_at(RING - 1 - step)
        landed(place).wait_recv()
        decode_at(place)

    to_next.wait_send()
    to_prev.wait_send()

    @pl.loop(1, RING)
    def _(step):
        place = lax.rem(me + step, RING)
        share(place).wait_send()
        spread(place).wait_send()


def local(momentum):
    rows, cols = momentum.shape[2:]
    table = jnp.asarray(tables())
    kept = cols // TILE * KEEP // RING
    vmem = pl.BlockSpec(memory_space=pltpu.VMEM)
    block = (KEEP, kept)
    dma = pltpu.SemaphoreType.DMA
    return pl.pallas_call(
        kernel,
        out_shape=(
            pltpu.VMEM(momentum.shape, F32),
            pltpu.VMEM((1, rows, cols), BF16),
        ),
        in_specs=[pl.BlockSpec(memory_space=pltpu.HBM)] * 2,
        out_specs=(vmem, vmem),
        scratch_shapes=[
            pltpu.VMEM((rows, cols), F32),
            pltpu.VMEM(table.shape, F32),
            pltpu.VMEM((512, 256), BF16),
            pltpu.VMEM((16, 192), BF16),
            pltpu.VMEM((384, 512), BF16),
            pltpu.VMEM((64, 48), BF16),
            pltpu.VMEM((RING, *block), F32),
            pltpu.VMEM((RING, *block), F32),
            pltpu.VMEM((2, *block), F32),
            pltpu.VMEM((2, *block), F32),
            pltpu.VMEM((2, *block), F32),
            pltpu.VMEM((RING, *block), F32),
            dma((RING,)),
            dma,
            dma((RING,)),
            dma((RING,)),
            dma((2,)),
            dma((2,)),
            dma((RING,)),
            dma((RING,)),
        ],
        compiler_params=pltpu.CompilerParams(
            collective_id=0, has_side_effects=True, vmem_limit_bytes=60 * 1024 * 1024),
    )(momentum, table)


def solution(mesh):
    in_specs = (P("outer", "rep", "shard", None),)
    out_specs = (P("outer", "rep", "shard", None), P("outer", "shard", None))
    return jax.shard_map(local, mesh=mesh, in_specs=in_specs, out_specs=out_specs, check_vma=False)
```

```python
import functools

import jax
import jax.numpy as jnp
import ml_dtypes
import numpy as np
from jax import lax
from jax.experimental import pallas as pl
from jax.experimental.pallas import tpu as pltpu
from jax.sharding import PartitionSpec as P

TILE = 64
KEEP = 16
RING = 8
POD = 4
GROUP = 8
MESH = pl.DeviceIdType.MESH
BF16 = jnp.bfloat16
F32 = jnp.float32


def low_basis():
    index = np.arange(TILE)
    freq = np.arange(KEEP)
    angles = np.pi * (2.0 * index[None, :] + 1.0) * freq[:, None] / (2.0 * TILE)
    scales = np.where(freq == 0, np.sqrt(1.0 / TILE), np.sqrt(2.0 / TILE))
    return (scales[:, None] * np.cos(angles)).astype(np.float32)


def halves(array):
    high = array.astype(ml_dtypes.bfloat16)
    low = (array - high.astype(np.float32)).astype(ml_dtypes.bfloat16)
    return high, low


def tables():
    basis = low_basis()
    high, low = (half.astype(np.float32) for half in halves(basis))
    out = np.zeros((208, 256), np.float32)
    out[:128, :128] = np.tile(basis, (GROUP, 2))
    out[:128, 128:] = np.tile(basis.T, (2, GROUP))
    out[128:144, :192] = np.concatenate([high, low, high], axis=1)
    out[144:, :48] = np.concatenate([high.T, high.T, low.T], axis=1)
    return out


def set_up(table, enc_cols, enc_rows, dec_cols, dec_rows):
    for place in range(4):
        lanes = pl.ds(place * 128, 128)
        row = lax.broadcasted_iota(jnp.int32, (128, 128), 0)
        col = lax.broadcasted_iota(jnp.int32, (128, 128), 1)
        high, low = split(jnp.where(row // KEEP == 2 * place + col // TILE, table[:128, :128], 0.0))
        dec_cols[:128, lanes] = high
        dec_cols[128:256, lanes] = high
        dec_cols[256:, lanes] = low
        high, low = split(jnp.where(col // KEEP == 2 * place + row // TILE, table[:128, 128:], 0.0))
        enc_cols[lanes, :128] = high
        enc_cols[lanes, 128:] = low
    enc_rows[...] = table[128:144, :192].astype(BF16)
    dec_rows[...] = table[144:, :48].astype(BF16)


def split(value):
    high = value.astype(BF16)
    low = (value - high.astype(F32)).astype(BF16)
    return high, low


def dot(a, b):
    return jnp.dot(a, b, preferred_element_type=F32)


def encode(groups, enc_cols, enc_rows):
    high, low = split(jnp.concatenate(groups, axis=0))
    both = dot(high, enc_cols[...])
    right = both[:, :128] + both[:, 128:] + dot(low, enc_cols[:, :128])
    right = jnp.concatenate([right[g * TILE:(g + 1) * TILE] for g in range(len(groups))], axis=1)
    high, low = split(right)
    return dot(enc_rows[...], jnp.concatenate([high, high, low], axis=0))


def decode(blocks, dec_cols, dec_rows, put):
    high, low = split(jnp.concatenate(blocks, axis=0))
    right = dot(jnp.concatenate([high, low, high], axis=1), dec_cols[...])
    for g in range(len(blocks)):
        high, low = split(right[g * KEEP:(g + 1) * KEEP])
        put(g, dot(dec_rows[...], jnp.concatenate([high, low, high], axis=0)))


def kernel(x_hbm, table_hbm, fresh, update,
           x, table, enc_cols, enc_rows, dec_cols, dec_rows, coeffs, parts, sums, around, mixed, got,
           x_sem, table_sem, rs_send, rs_recv, swap_send, swap_recv, ag_send, ag_recv):
    outer, rep, shard = (lax.axis_index(axis) for axis in ("outer", "rep", "shard"))
    columns = lax.axis_size("outer") // 2
    column, side, core = outer // 2, outer % 2, shard % 2
    me = side * POD + rep
    wide = GROUP * TILE

    def ring(place, to_core):
        return {"outer": column * 2 + place // POD, "rep": place % POD, "shard": shard - core + to_core}

    def beside(step):
        return {"outer": lax.rem(column + step + columns, columns) * 2 + side}

    def place_at(step):
        half = (step + 1) // 2
        return lax.rem(me + 4 + half * (1 - 2 * (step % 2)), RING)

    def load(part):
        cols = pl.ds(part * 2 * wide, 2 * wide)
        return pltpu.make_async_copy(x_hbm.at[0, 0, :, cols], x.at[:, cols], x_sem.at[part])

    table_copy = pltpu.make_async_copy(table_hbm, table, table_sem)
    table_copy.start()
    for part in range(RING):
        load(part).start()

    barrier = pltpu.get_barrier_semaphore()
    for step in range(RING):
        @pl.when((core == 0) | (step > 0))
        def _():
            pl.semaphore_signal(
                barrier, inc=1, device_id=ring(lax.rem(me + step, RING), 1), device_id_type=MESH)

    @pl.when(core == 1)
    def _():
        for step in range(RING):
            pl.semaphore_signal(
                barrier, inc=1, device_id=ring(lax.rem(me + step, RING), 0), device_id_type=MESH)
        for step in (1, -1):
            pl.semaphore_signal(barrier, inc=1, device_id=beside(step), device_id_type=MESH)

    def share(half, place):
        return pltpu.make_async_remote_copy(
            src_ref=coeffs.at[half, place], dst_ref=parts.at[half, side, core * POD + rep],
            send_sem=rs_send, recv_sem=rs_recv.at[half, side],
            device_id=ring(place, 1), device_id_type=MESH)

    def swap(half, pod):
        return pltpu.make_async_remote_copy(
            src_ref=sums.at[half, pod], dst_ref=around.at[half, pod],
            send_sem=swap_send.at[half, pod], recv_sem=swap_recv.at[half, pod],
            device_id=beside(2 * pod - 1), device_id_type=MESH)

    def spread(half, to_core, place):
        return pltpu.make_async_remote_copy(
            src_ref=mixed.at[half, place // POD, to_core], dst_ref=got.at[half, me],
            send_sem=ag_send, recv_sem=ag_recv.at[half],
            device_id=ring(place, to_core), device_id_type=MESH)

    def bytes_of(blocks, sem):
        return pltpu.make_async_copy(parts.at[0, 0, pl.ds(0, blocks)], parts.at[0, 0, pl.ds(0, blocks)], sem)

    table_copy.wait()
    set_up(table, enc_cols, enc_rows, dec_cols, dec_rows)

    for half in range(2):
        for part in range(4):
            load(half * 4 + part).wait()
        groups = [x[:, pl.ds((half * RING + g) * wide, wide)] for g in range(RING)]
        out = encode(groups, enc_cols, enc_rows)
        for g in range(RING):
            coeffs[half, g] = out[:, g * 128:(g + 1) * 128]

    @pl.when(core == 0)
    def _():
        pl.semaphore_wait(barrier, RING)

    @pl.when(core == 1)
    def _():
        pl.semaphore_wait(barrier, 2 * RING + 1)
        for half in range(2):
            parts[half, side, POD + rep] = coeffs[half, me]

    for half in range(2):
        @pl.loop(0, RING - core)
        def _(step):
            share(half, place_at(step)).start()

    def put_fresh(g, value):
        cols = pl.ds(g * wide, wide)
        fresh[0, 0, :, cols] = x[:, cols] - value

    decode([coeffs[half, g] for half in range(2) for g in range(RING)], dec_cols, dec_rows, put_fresh)

    @pl.when(core == 1)
    def _():
        for half in range(2):
            for pod, blocks in ((side, RING - 1), (1 - side, RING)):
                bytes_of(blocks, rs_recv.at[half, pod]).wait()
                for of_core in range(2):
                    terms = [parts[half, pod, of_core * POD + r] for r in range(POD)]
                    sums[half, pod, of_core] = (terms[0] + terms[1]) + (terms[2] + terms[3])
                swap(half, pod).start()

        for half in range(2):
            for pod in range(2):
                swap(half, pod).wait_recv()
            for pod in range(2):
                mixed[half, pod] = 0.5 * sums[half, pod] + 0.25 * (sums[half, 1 - pod] + around[half, 1 - pod])
            for to_core in range(2):
                @pl.loop(0, RING - to_core)
                def _(step):
                    spread(half, to_core, place_at(step)).start()
            got[half, me] = mixed[half, side, 1]

        for half in range(2):
            bytes_of(RING - 1, rs_send).wait()
            for pod in range(2):
                swap(half, pod).wait_send()

    @pl.when(core == 0)
    def _():
        for half in range(2):
            bytes_of(RING, rs_send).wait()

    for half in range(2):
        @pl.when(core == 0)
        def _():
            bytes_of(RING, ag_recv.at[half]).wait()

        @pl.when(core == 1)
        def _():
            bytes_of(RING - 1, ag_recv.at[half]).wait()

        def put_update(g, value):
            update[0, :, pl.ds((half * RING + g) * wide, wide)] = value.astype(BF16)

        decode([got[half, g] for g in range(RING)], dec_cols, dec_rows, put_update)

    @pl.when(core == 1)
    def _():
        for half in range(2):
            for to_core in range(2):
                bytes_of(RING - to_core, ag_send).wait()


def write_out(fresh_in, update_in, fresh, update, sems):
    copies = [pltpu.make_async_copy(fresh_in, fresh, sems.at[0]), pltpu.make_async_copy(update_in, update, sems.at[1])]
    for copy in copies:
        copy.start()
    for copy in copies:
        copy.wait()


def local(momentum):
    rows, cols = momentum.shape[2:]
    table = jnp.asarray(tables())
    vmem = pl.BlockSpec(memory_space=pltpu.VMEM)
    anywhere = pl.BlockSpec(memory_space=pl.ANY)
    block = (KEEP, GROUP * KEEP)
    dma = pltpu.SemaphoreType.DMA
    fresh, update = pl.pallas_call(
        kernel,
        out_shape=(
            pltpu.VMEM(momentum.shape, F32),
            pltpu.VMEM((1, rows, cols), BF16),
        ),
        in_specs=[pl.BlockSpec(memory_space=pltpu.HBM)] * 2,
        out_specs=(vmem, vmem),
        scratch_shapes=[
            pltpu.VMEM((rows, cols), F32),
            pltpu.VMEM(table.shape, F32),
            pltpu.VMEM((512, 256), BF16),
            pltpu.VMEM((16, 192), BF16),
            pltpu.VMEM((384, 512), BF16),
            pltpu.VMEM((64, 48), BF16),
            pltpu.VMEM((2, RING, *block), F32),
            pltpu.VMEM((2, 2, RING, *block), F32),
            pltpu.VMEM((2, 2, 2, *block), F32),
            pltpu.VMEM((2, 2, 2, *block), F32),
            pltpu.VMEM((2, 2, 2, *block), F32),
            pltpu.VMEM((2, RING, *block), F32),
            dma((RING,)),
            dma,
            dma,
            dma((2, 2)),
            dma((2, 2)),
            dma((2, 2)),
            dma,
            dma((2,)),
        ],
        compiler_params=pltpu.CompilerParams(
            collective_id=0, has_side_effects=True, vmem_limit_bytes=60 * 1024 * 1024),
    )(momentum, table)
    return pl.pallas_call(
        write_out,
        out_shape=(jax.ShapeDtypeStruct(fresh.shape, F32), jax.ShapeDtypeStruct(update.shape, BF16)),
        in_specs=[anywhere] * 2,
        out_specs=(anywhere,) * 2,
        scratch_shapes=[dma((2,))],
        compiler_params=pltpu.CompilerParams(vmem_limit_bytes=8 * 1024 * 1024),
    )(fresh, update)


def solution(mesh):
    in_specs = (P("outer", "rep", "shard", None),)
    out_specs = (P("outer", "rep", "shard", None), P("outer", "shard", None))
    return jax.shard_map(local, mesh=mesh, in_specs=in_specs, out_specs=out_specs, check_vma=False)
```

```python
import functools

import jax
import jax.numpy as jnp
import ml_dtypes
import numpy as np
from jax import lax
from jax.experimental import pallas as pl
from jax.experimental.pallas import tpu as pltpu
from jax.sharding import PartitionSpec as P

TILE = 64
KEEP = 16
RING = 8
POD = 4
GROUP = 8
LOGICAL = pl.DeviceIdType.LOGICAL
BF16 = jnp.bfloat16
F32 = jnp.float32


def low_basis():
    index = np.arange(TILE)
    freq = np.arange(KEEP)
    angles = np.pi * (2.0 * index[None, :] + 1.0) * freq[:, None] / (2.0 * TILE)
    scales = np.where(freq == 0, np.sqrt(1.0 / TILE), np.sqrt(2.0 / TILE))
    return (scales[:, None] * np.cos(angles)).astype(np.float32)


def halves(array):
    high = array.astype(ml_dtypes.bfloat16)
    low = (array - high.astype(np.float32)).astype(ml_dtypes.bfloat16)
    return high, low


def tables():
    basis = low_basis()
    high, low = (half.astype(np.float32) for half in halves(basis))
    out = np.zeros((208, 256), np.float32)
    out[:128, :128] = np.tile(basis, (GROUP, 2))
    out[:128, 128:] = np.tile(basis.T, (2, GROUP))
    out[128:144, :192] = np.concatenate([high, low, high], axis=1)
    out[144:, :48] = np.concatenate([high.T, high.T, low.T], axis=1)
    return out


def set_up(table, enc_cols, enc_rows, dec_cols, dec_rows):
    for place in range(4):
        lanes = pl.ds(place * 128, 128)
        row = lax.broadcasted_iota(jnp.int32, (128, 128), 0)
        col = lax.broadcasted_iota(jnp.int32, (128, 128), 1)
        high, low = split(jnp.where(row // KEEP == 2 * place + col // TILE, table[:128, :128], 0.0))
        dec_cols[:128, lanes] = high
        dec_cols[128:256, lanes] = high
        dec_cols[256:, lanes] = low
        high, low = split(jnp.where(col // KEEP == 2 * place + row // TILE, table[:128, 128:], 0.0))
        enc_cols[lanes, :128] = high
        enc_cols[lanes, 128:] = low
    enc_rows[...] = table[128:144, :192].astype(BF16)
    dec_rows[...] = table[144:, :48].astype(BF16)


def split(value):
    high = value.astype(BF16)
    low = (value - high.astype(F32)).astype(BF16)
    return high, low


def dot(a, b):
    return jnp.dot(a, b, preferred_element_type=F32)


def encode(groups, enc_cols, enc_rows):
    high, low = split(jnp.concatenate(groups, axis=0))
    both = dot(high, enc_cols[...])
    right = both[:, :128] + both[:, 128:] + dot(low, enc_cols[:, :128])
    right = jnp.concatenate([right[g * TILE:(g + 1) * TILE] for g in range(len(groups))], axis=1)
    high, low = split(right)
    return dot(enc_rows[...], jnp.concatenate([high, high, low], axis=0))


def decode(blocks, dec_cols, dec_rows, put):
    high, low = split(jnp.concatenate(blocks, axis=0))
    right = dot(jnp.concatenate([high, low, high], axis=1), dec_cols[...])
    for g in range(len(blocks)):
        high, low = split(right[g * KEEP:(g + 1) * KEEP])
        put(g, dot(dec_rows[...], jnp.concatenate([high, low, high], axis=0)))


def kernel(x_hbm, table_hbm, fresh, update, later, dec_cols, dec_rows,
           x, table, enc_cols, enc_rows, coeffs, parts, sums, around, mixed, got,
           x_sem, table_sem, rs_send, rs_recv, swap_send, swap_recv, ag_send, ag_recv):
    outer, rep, shard = (lax.axis_index(axis) for axis in ("outer", "rep", "shard"))
    columns = lax.axis_size("outer") // 2
    column, side, core = outer // 2, outer % 2, shard % 2
    me = side * POD + rep
    wide = GROUP * TILE

    places = [lax.rem(me + ahead, RING) for ahead in (4, 3, 5, 2, 6, 1, 7, 0)]
    n_shard = lax.axis_size("shard")
    here = shard - core
    targets = [((column * 2 + place // POD) * POD + place % POD) * n_shard + here for place in places]
    pods = [place // POD for place in places]

    def beside(pod):
        to = lax.rem(column + 2 * pod - 1 + columns, columns)
        return ((to * 2 + side) * POD + rep) * n_shard + here + 1

    def load(part):
        cols = pl.ds(part * 2 * wide, 2 * wide)
        return pltpu.make_async_copy(x_hbm.at[0, 0, :, cols], x.at[:, cols], x_sem.at[part])

    table_copy = pltpu.make_async_copy(table_hbm, table, table_sem)
    table_copy.start()
    for part in range(RING):
        load(part).start()

    barrier = pltpu.get_barrier_semaphore()

    def signal(device):
        pl.semaphore_signal(barrier, inc=1, device_id=device, device_id_type=LOGICAL)

    for target in targets[:-1]:
        signal(target + 1)

    @pl.when(core == 0)
    def _():
        signal(targets[-1] + 1)

    @pl.when(core == 1)
    def _():
        for target in targets:
            signal(target)
        for pod in range(2):
            signal(beside(pod))

    def share(half, step):
        return pltpu.make_async_remote_copy(
            src_ref=coeffs.at[half, places[step]], dst_ref=parts.at[half, side, core * POD + rep],
            send_sem=rs_send, recv_sem=rs_recv.at[half, side],
            device_id=targets[step] + 1, device_id_type=LOGICAL)

    def swap(half, pod):
        return pltpu.make_async_remote_copy(
            src_ref=sums.at[half, pod], dst_ref=around.at[half, pod],
            send_sem=swap_send.at[half, pod], recv_sem=swap_recv.at[half, pod],
            device_id=beside(pod), device_id_type=LOGICAL)

    def spread(half, to_core, step):
        return pltpu.make_async_remote_copy(
            src_ref=mixed.at[half, pods[step], to_core], dst_ref=got.at[half, me],
            send_sem=ag_send, recv_sem=ag_recv.at[half],
            device_id=targets[step] + to_core, device_id_type=LOGICAL)

    def bytes_of(blocks, sem):
        return pltpu.make_async_copy(parts.at[0, 0, pl.ds(0, blocks)], parts.at[0, 0, pl.ds(0, blocks)], sem)

    table_copy.wait()
    set_up(table, enc_cols, enc_rows, dec_cols, dec_rows)

    for half in range(2):
        for part in range(4):
            load(half * 4 + part).wait()
        groups = [x[:, pl.ds((half * RING + g) * wide, wide)] for g in range(RING)]
        out = encode(groups, enc_cols, enc_rows)
        for g in range(RING):
            coeffs[half, g] = out[:, g * 128:(g + 1) * 128]

        if half == 0:
            @pl.when(core == 0)
            def _():
                pl.semaphore_wait(barrier, RING)

            @pl.when(core == 1)
            def _():
                pl.semaphore_wait(barrier, 2 * RING + 1)

        for step in range(RING - 1):
            share(half, step).start()

        @pl.when(core == 0)
        def _():
            share(half, RING - 1).start()

        @pl.when(core == 1)
        def _():
            parts[half, side, POD + rep] = coeffs[half, me]

    def put_fresh(g, value):
        cols = pl.ds(g * wide, wide)
        fresh[0, 0, :, cols] = x[:, cols] - value

    decode([coeffs[half, g] for half in range(2) for g in range(RING)], dec_cols, dec_rows, put_fresh)

    @pl.when(core == 1)
    def _():
        for half in range(2):
            for pod, blocks in ((side, RING - 1), (1 - side, RING)):
                bytes_of(blocks, rs_recv.at[half, pod]).wait()
                for of_core in range(2):
                    terms = [parts[half, pod, of_core * POD + r] for r in range(POD)]
                    sums[half, pod, of_core] = (terms[0] + terms[1]) + (terms[2] + terms[3])
                swap(half, pod).start()

        for half in range(2):
            for pod in range(2):
                swap(half, pod).wait_recv()
            for pod in range(2):
                mixed[half, pod] = 0.5 * sums[half, pod] + 0.25 * (sums[half, 1 - pod] + around[half, 1 - pod])
            for to_core in range(2):
                for step in range(RING - to_core):
                    spread(half, to_core, step).start()
            got[half, me] = mixed[half, side, 1]

        for half in range(2):
            bytes_of(RING - 1, rs_send).wait()
            for pod in range(2):
                swap(half, pod).wait_send()

    @pl.when(core == 0)
    def _():
        for half in range(2):
            bytes_of(RING, rs_send).wait()

    for half in range(2):
        @pl.when(core == 0)
        def _():
            bytes_of(RING, ag_recv.at[half]).wait()

        @pl.when(core == 1)
        def _():
            bytes_of(RING - 1, ag_recv.at[half]).wait()

        if half == 0:
            def put_update(g, value):
                update[:, pl.ds(g * wide, wide)] = value.astype(BF16)

            decode([got[0, g] for g in range(RING)], dec_cols, dec_rows, put_update)
        else:
            later[...] = got[1]

    @pl.when(core == 1)
    def _():
        for half in range(2):
            for to_core in range(2):
                bytes_of(RING - to_core, ag_send).wait()


def finish(fresh_in, update_in, later, dec_cols, dec_rows, fresh, update, second, sems):
    half = second.shape[1]
    copies = [
        pltpu.make_async_copy(fresh_in, fresh, sems.at[0]),
        pltpu.make_async_copy(update_in, update.at[0, :, pl.ds(0, half)], sems.at[1]),
    ]
    for copy in copies:
        copy.start()

    def put(g, value):
        second[:, pl.ds(g * GROUP * TILE, GROUP * TILE)] = value.astype(BF16)

    decode([later[g] for g in range(RING)], dec_cols, dec_rows, put)
    copies.append(pltpu.make_async_copy(second, update.at[0, :, pl.ds(half, half)], sems.at[2]))
    copies[-1].start()
    for copy in copies:
        copy.wait()


def local(momentum):
    rows, cols = momentum.shape[2:]
    table = jnp.asarray(tables())
    vmem = pl.BlockSpec(memory_space=pltpu.VMEM)
    anywhere = pl.BlockSpec(memory_space=pl.ANY)
    block = (KEEP, GROUP * KEEP)
    dma = pltpu.SemaphoreType.DMA
    fresh, *rest = pl.pallas_call(
        kernel,
        out_shape=(
            pltpu.VMEM(momentum.shape, F32),
            pltpu.VMEM((rows, cols // 2), BF16),
            pltpu.VMEM((RING, *block), F32),
            pltpu.VMEM((384, 512), BF16),
            pltpu.VMEM((64, 48), BF16),
        ),
        in_specs=[pl.BlockSpec(memory_space=pltpu.HBM)] * 2,
        out_specs=(vmem,) * 5,
        scratch_shapes=[
            pltpu.VMEM((rows, cols), F32),
            pltpu.VMEM(table.shape, F32),
            pltpu.VMEM((512, 256), BF16),
            pltpu.VMEM((16, 192), BF16),
            pltpu.VMEM((2, RING, *block), F32),
            pltpu.VMEM((2, 2, RING, *block), F32),
            pltpu.VMEM((2, 2, 2, *block), F32),
            pltpu.VMEM((2, 2, 2, *block), F32),
            pltpu.VMEM((2, 2, 2, *block), F32),
            pltpu.VMEM((2, RING, *block), F32),
            dma((RING,)),
            dma,
            dma,
            dma((2, 2)),
            dma((2, 2)),
            dma((2, 2)),
            dma,
            dma((2,)),
        ],
        compiler_params=pltpu.CompilerParams(
            collective_id=0, has_side_effects=True, vmem_limit_bytes=60 * 1024 * 1024),
    )(momentum, table)
    return pl.pallas_call(
        finish,
        out_shape=(jax.ShapeDtypeStruct(fresh.shape, F32), jax.ShapeDtypeStruct((1, rows, cols), BF16)),
        in_specs=[anywhere] * 2 + [vmem] * 3,
        out_specs=(anywhere,) * 2,
        scratch_shapes=[pltpu.VMEM((rows, cols // 2), BF16), dma((3,))],
        compiler_params=pltpu.CompilerParams(vmem_limit_bytes=16 * 1024 * 1024),
    )(fresh, *rest)


def solution(mesh):
    in_specs = (P("outer", "rep", "shard", None),)
    out_specs = (P("outer", "rep", "shard", None), P("outer", "shard", None))
    return jax.shard_map(local, mesh=mesh, in_specs=in_specs, out_specs=out_specs, check_vma=False)
```

```python
import functools

import jax
import jax.numpy as jnp
import ml_dtypes
import numpy as np
from jax import lax
from jax.experimental import pallas as pl
from jax.experimental.pallas import tpu as pltpu
from jax.sharding import PartitionSpec as P

TILE = 64
KEEP = 16
RING = 8
POD = 4
GROUP = 8
LOGICAL = pl.DeviceIdType.LOGICAL
BF16 = jnp.bfloat16
F32 = jnp.float32


def low_basis():
    index = np.arange(TILE)
    freq = np.arange(KEEP)
    angles = np.pi * (2.0 * index[None, :] + 1.0) * freq[:, None] / (2.0 * TILE)
    scales = np.where(freq == 0, np.sqrt(1.0 / TILE), np.sqrt(2.0 / TILE))
    return (scales[:, None] * np.cos(angles)).astype(np.float32)


def halves(array):
    high = array.astype(ml_dtypes.bfloat16)
    low = (array - high.astype(np.float32)).astype(ml_dtypes.bfloat16)
    return high, low


def tables():
    basis = low_basis()
    high, low = (half.astype(np.float32) for half in halves(basis))
    out = np.zeros((208, 256), np.float32)
    out[:128, :128] = np.tile(basis, (GROUP, 2))
    out[:128, 128:] = np.tile(basis.T, (2, GROUP))
    out[128:144, :192] = np.concatenate([high, low, high], axis=1)
    out[144:, :48] = np.concatenate([high.T, high.T, low.T], axis=1)
    return out


def encode_operands(table, enc_cols, enc_rows):
    row = lax.broadcasted_iota(jnp.int32, (128, 128), 0)
    col = lax.broadcasted_iota(jnp.int32, (128, 128), 1)
    for place in range(4):
        lanes = pl.ds(place * 128, 128)
        high, low = split(jnp.where(col // KEEP == 2 * place + row // TILE, table[:128, 128:], 0.0))
        enc_cols[lanes, :128] = high
        enc_cols[lanes, 128:] = low
    enc_rows[...] = table[128:144, :192].astype(BF16)


def decode_operands(table, dec_cols, dec_rows):
    row = lax.broadcasted_iota(jnp.int32, (128, 128), 0)
    col = lax.broadcasted_iota(jnp.int32, (128, 128), 1)
    for place in range(4):
        lanes = pl.ds(place * 128, 128)
        high, low = split(jnp.where(row // KEEP == 2 * place + col // TILE, table[:128, :128], 0.0))
        dec_cols[:128, lanes] = high
        dec_cols[128:256, lanes] = high
        dec_cols[256:, lanes] = low
    dec_rows[...] = table[144:, :48].astype(BF16)


def split(value):
    high = value.astype(BF16)
    low = (value - high.astype(F32)).astype(BF16)
    return high, low


def dot(a, b):
    return jnp.dot(a, b, preferred_element_type=F32)


def encode(groups, enc_cols, enc_rows):
    high, low = split(jnp.concatenate(groups, axis=0))
    both = dot(high, enc_cols[...])
    right = both[:, :128] + both[:, 128:] + dot(low, enc_cols[:, :128])
    right = jnp.concatenate([right[g * TILE:(g + 1) * TILE] for g in range(len(groups))], axis=1)
    high, low = split(right)
    return dot(enc_rows[...], jnp.concatenate([high, high, low], axis=0))


def decode(blocks, dec_cols, dec_rows, put):
    high, low = split(jnp.concatenate(blocks, axis=0))
    right = dot(jnp.concatenate([high, low, high], axis=1), dec_cols[...])
    for g in range(len(blocks)):
        high, low = split(right[g * KEEP:(g + 1) * KEEP])
        put(g, dot(dec_rows[...], jnp.concatenate([high, low, high], axis=0)))


def kernel(x_hbm, table_hbm, fresh, update, later, dec_cols, dec_rows,
           x, table, enc_cols, enc_rows, coeffs, parts, sums, around, mixed, got,
           x_sem, table_sem, rs_send, rs_recv, swap_send, swap_recv, ag_send, ag_recv):
    outer, rep, shard = (lax.axis_index(axis) for axis in ("outer", "rep", "shard"))
    columns = lax.axis_size("outer") // 2
    column, side, core = outer // 2, outer % 2, shard % 2
    me = side * POD + rep
    wide = GROUP * TILE

    n_shard = lax.axis_size("shard")
    here = shard - core

    def target(place):
        return ((column * 2 + place // POD) * POD + place % POD) * n_shard + here

    places = [lax.rem(me + ahead, RING) for ahead in (4, 3, 5, 2, 6, 1, 7, 0)]
    targets = [target(place) for place in places]

    def beside(pod):
        to = lax.rem(column + 2 * pod - 1 + columns, columns)
        return ((to * 2 + side) * POD + rep) * n_shard + here + 1

    def load(part):
        cols = pl.ds(part * 2 * wide, 2 * wide)
        return pltpu.make_async_copy(x_hbm.at[0, 0, :, cols], x.at[:, cols], x_sem.at[part])

    table_copy = pltpu.make_async_copy(table_hbm, table, table_sem)
    table_copy.start()
    for part in range(RING):
        load(part).start()

    barrier = pltpu.get_barrier_semaphore()

    def signal(device):
        pl.semaphore_signal(barrier, inc=1, device_id=device, device_id_type=LOGICAL)

    for device in targets[:-1]:
        signal(device + 1)

    @pl.when(core == 0)
    def _():
        signal(targets[-1] + 1)

    @pl.when(core == 1)
    def _():
        for device in targets:
            signal(device)
        for pod in range(2):
            signal(beside(pod))

    def share(half, step):
        return pltpu.make_async_remote_copy(
            src_ref=coeffs.at[half, places[step]], dst_ref=parts.at[half, core, side, rep],
            send_sem=rs_send, recv_sem=rs_recv.at[half, core, side],
            device_id=targets[step] + 1, device_id_type=LOGICAL)

    def swap(half, of_core, pod):
        return pltpu.make_async_remote_copy(
            src_ref=sums.at[half, of_core, pod], dst_ref=around.at[half, of_core, pod],
            send_sem=swap_send, recv_sem=swap_recv.at[half, of_core, pod],
            device_id=beside(pod), device_id_type=LOGICAL)

    def spread(half, to_core, pod, ahead):
        place = pod * POD + lax.rem(rep + ahead, POD)
        return pltpu.make_async_remote_copy(
            src_ref=mixed.at[half, to_core, pod], dst_ref=got.at[half, me],
            send_sem=ag_send, recv_sem=ag_recv.at[half],
            device_id=target(place) + to_core, device_id_type=LOGICAL)

    def bytes_of(blocks, sem):
        some = coeffs.at[0, pl.ds(0, blocks)]
        return pltpu.make_async_copy(some, some, sem)

    table_copy.wait()
    encode_operands(table, enc_cols, enc_rows)

    for half in range(2):
        for part in range(4):
            load(half * 4 + part).wait()
        groups = [x[:, pl.ds((half * RING + g) * wide, wide)] for g in range(RING)]
        out = encode(groups, enc_cols, enc_rows)
        for g in range(RING):
            coeffs[half, g] = out[:, g * 128:(g + 1) * 128]

        if half == 0:
            @pl.when(core == 0)
            def _():
                pl.semaphore_wait(barrier, RING)

            @pl.when(core == 1)
            def _():
                pl.semaphore_wait(barrier, 2 * RING + 1)

        for step in range(RING - 1):
            share(half, step).start()

        @pl.when(core == 0)
        def _():
            share(half, RING - 1).start()

        @pl.when(core == 1)
        def _():
            parts[half, 1, side, rep] = coeffs[half, me]

    def put_fresh(g, value):
        cols = pl.ds(g * wide, wide)
        fresh[0, 0, :, cols] = x[:, cols] - value

    decode_operands(table, dec_cols, dec_rows)
    decode([coeffs[half, g] for half in range(2) for g in range(RING)], dec_cols, dec_rows, put_fresh)

    @pl.when(core == 1)
    def _():
        for half in range(2):
            for of_core in (1, 0):
                for pod, own in ((side, 1), (1 - side, 0)):
                    bytes_of(POD - own * of_core, rs_recv.at[half, of_core, pod]).wait()
                    terms = [parts[half, of_core, pod, r] for r in range(POD)]
                    sums[half, of_core, pod] = (terms[0] + terms[1]) + (terms[2] + terms[3])
                    swap(half, of_core, pod).start()

        for half in range(2):
            for of_core in (1, 0):
                for pod in range(2):
                    swap(half, of_core, 1 - pod).wait_recv()
                    mixed[half, of_core, pod] = 0.5 * sums[half, of_core, pod] + 0.25 * (
                        sums[half, of_core, 1 - pod] + around[half, of_core, 1 - pod])
                    if of_core == 0:
                        spread(half, of_core, pod, 0).start()
                    else:
                        @pl.when(pod != side)
                        def _():
                            spread(half, of_core, pod, 0).start()

                        @pl.when(pod == side)
                        def _():
                            got[half, me] = mixed[half, of_core, pod]

                    for ahead in range(1, POD):
                        spread(half, of_core, pod, ahead).start()

        for half in range(2):
            bytes_of(RING - 1, rs_send).wait()
        bytes_of(RING, swap_send).wait()

    @pl.when(core == 0)
    def _():
        for half in range(2):
            bytes_of(RING, rs_send).wait()

    for half in range(2):
        @pl.when(core == 0)
        def _():
            bytes_of(RING, ag_recv.at[half]).wait()

        @pl.when(core == 1)
        def _():
            bytes_of(RING - 1, ag_recv.at[half]).wait()

        if half == 0:
            def put_update(g, value):
                update[:, pl.ds(g * wide, wide)] = value.astype(BF16)

            decode([got[0, g] for g in range(RING)], dec_cols, dec_rows, put_update)
        else:
            later[...] = got[1]

    @pl.when(core == 1)
    def _():
        for half in range(2):
            for to_core in range(2):
                bytes_of(RING - to_core, ag_send).wait()


def finish(fresh_in, update_in, later, dec_cols, dec_rows, fresh, update, second, sems):
    half = second.shape[1]
    copies = [
        pltpu.make_async_copy(fresh_in, fresh, sems.at[0]),
        pltpu.make_async_copy(update_in, update.at[0, :, pl.ds(0, half)], sems.at[1]),
    ]
    for copy in copies:
        copy.start()

    def put(g, value):
        second[:, pl.ds(g * GROUP * TILE, GROUP * TILE)] = value.astype(BF16)

    decode([later[g] for g in range(RING)], dec_cols, dec_rows, put)
    copies.append(pltpu.make_async_copy(second, update.at[0, :, pl.ds(half, half)], sems.at[2]))
    copies[-1].start()
    for copy in copies:
        copy.wait()


def local(momentum):
    rows, cols = momentum.shape[2:]
    table = jnp.asarray(tables())
    vmem = pl.BlockSpec(memory_space=pltpu.VMEM)
    anywhere = pl.BlockSpec(memory_space=pl.ANY)
    block = (KEEP, GROUP * KEEP)
    dma = pltpu.SemaphoreType.DMA
    fresh, *rest = pl.pallas_call(
        kernel,
        out_shape=(
            pltpu.VMEM(momentum.shape, F32),
            pltpu.VMEM((rows, cols // 2), BF16),
            pltpu.VMEM((RING, *block), F32),
            pltpu.VMEM((384, 512), BF16),
            pltpu.VMEM((64, 48), BF16),
        ),
        in_specs=[pl.BlockSpec(memory_space=pltpu.HBM)] * 2,
        out_specs=(vmem,) * 5,
        scratch_shapes=[
            pltpu.VMEM((rows, cols), F32),
            pltpu.VMEM(table.shape, F32),
            pltpu.VMEM((512, 256), BF16),
            pltpu.VMEM((16, 192), BF16),
            pltpu.VMEM((2, RING, *block), F32),
            pltpu.VMEM((2, 2, 2, POD, *block), F32),
            pltpu.VMEM((2, 2, 2, *block), F32),
            pltpu.VMEM((2, 2, 2, *block), F32),
            pltpu.VMEM((2, 2, 2, *block), F32),
            pltpu.VMEM((2, RING, *block), F32),
            dma((RING,)),
            dma,
            dma,
            dma((2, 2, 2)),
            dma,
            dma((2, 2, 2)),
            dma,
            dma((2,)),
        ],
        compiler_params=pltpu.CompilerParams(
            collective_id=0, has_side_effects=True, vmem_limit_bytes=60 * 1024 * 1024),
    )(momentum, table)
    return pl.pallas_call(
        finish,
        out_shape=(jax.ShapeDtypeStruct(fresh.shape, F32), jax.ShapeDtypeStruct((1, rows, cols), BF16)),
        in_specs=[anywhere] * 2 + [vmem] * 3,
        out_specs=(anywhere,) * 2,
        scratch_shapes=[pltpu.VMEM((rows, cols // 2), BF16), dma((3,))],
        compiler_params=pltpu.CompilerParams(vmem_limit_bytes=16 * 1024 * 1024),
    )(fresh, *rest)


def solution(mesh):
    in_specs = (P("outer", "rep", "shard", None),)
    out_specs = (P("outer", "rep", "shard", None), P("outer", "shard", None))
    return jax.shard_map(local, mesh=mesh, in_specs=in_specs, out_specs=out_specs, check_vma=False)
```

```python
import functools

import jax
import jax.numpy as jnp
import ml_dtypes
import numpy as np
from jax import lax
from jax.experimental import pallas as pl
from jax.experimental.pallas import tpu as pltpu
from jax.sharding import PartitionSpec as P

TILE = 64
KEEP = 16
RING = 8
POD = 4
GROUP = 8
LOGICAL = pl.DeviceIdType.LOGICAL
BF16 = jnp.bfloat16
F32 = jnp.float32


def low_basis():
    index = np.arange(TILE)
    freq = np.arange(KEEP)
    angles = np.pi * (2.0 * index[None, :] + 1.0) * freq[:, None] / (2.0 * TILE)
    scales = np.where(freq == 0, np.sqrt(1.0 / TILE), np.sqrt(2.0 / TILE))
    return (scales[:, None] * np.cos(angles)).astype(np.float32)


def halves(array):
    high = array.astype(ml_dtypes.bfloat16)
    low = (array - high.astype(np.float32)).astype(ml_dtypes.bfloat16)
    return high, low


def tables():
    basis = low_basis()
    high, low = (half.astype(np.float32) for half in halves(basis))
    out = np.zeros((208, 256), np.float32)
    out[:128, :128] = np.tile(basis, (GROUP, 2))
    out[:128, 128:] = np.tile(basis.T, (2, GROUP))
    out[128:144, :192] = np.concatenate([high, low, high], axis=1)
    out[144:, :48] = np.concatenate([high.T, high.T, low.T], axis=1)
    return out


def encode_operands(table, enc_cols, enc_rows):
    row = lax.broadcasted_iota(jnp.int32, (128, 128), 0)
    col = lax.broadcasted_iota(jnp.int32, (128, 128), 1)
    for place in range(4):
        lanes = pl.ds(place * 128, 128)
        high, low = split(jnp.where(col // KEEP == 2 * place + row // TILE, table[:128, 128:], 0.0))
        enc_cols[lanes, :128] = high
        enc_cols[lanes, 128:] = low
    enc_rows[...] = table[128:144, :192].astype(BF16)


def decode_operands(table, dec_cols, dec_rows):
    row = lax.broadcasted_iota(jnp.int32, (128, 128), 0)
    col = lax.broadcasted_iota(jnp.int32, (128, 128), 1)
    for place in range(4):
        lanes = pl.ds(place * 128, 128)
        high, low = split(jnp.where(row // KEEP == 2 * place + col // TILE, table[:128, :128], 0.0))
        dec_cols[:128, lanes] = high
        dec_cols[128:256, lanes] = high
        dec_cols[256:, lanes] = low
    dec_rows[...] = table[144:, :48].astype(BF16)


def split(value):
    high = value.astype(BF16)
    low = (value - high.astype(F32)).astype(BF16)
    return high, low


def dot(a, b):
    return jnp.dot(a, b, preferred_element_type=F32)


def encode(groups, enc_cols, enc_rows):
    high, low = split(jnp.concatenate(groups, axis=0))
    both = dot(high, enc_cols[...])
    right = both[:, :128] + both[:, 128:] + dot(low, enc_cols[:, :128])
    right = jnp.concatenate([right[g * TILE:(g + 1) * TILE] for g in range(len(groups))], axis=1)
    high, low = split(right)
    return dot(enc_rows[...], jnp.concatenate([high, high, low], axis=0))


def decode(blocks, dec_cols, dec_rows, put):
    high, low = split(jnp.concatenate(blocks, axis=0))
    right = dot(jnp.concatenate([high, low, high], axis=1), dec_cols[...])
    for g in range(len(blocks)):
        high, low = split(right[g * KEEP:(g + 1) * KEEP])
        put(g, dot(dec_rows[...], jnp.concatenate([high, low, high], axis=0)))


def kernel(x_hbm, table_hbm, fresh, update, later, dec_cols, dec_rows,
           x, table, enc_cols, enc_rows, coeffs, parts, sums, around, mixed, got,
           x_sem, table_sem, rs_send, rs_recv, swap_send, swap_recv, ag_send, ag_recv):
    outer, rep, shard = (lax.axis_index(axis) for axis in ("outer", "rep", "shard"))
    columns = lax.axis_size("outer") // 2
    column, side, core = outer // 2, outer % 2, shard % 2
    me = side * POD + rep
    wide = GROUP * TILE

    n_shard = lax.axis_size("shard")
    here = shard - core

    def target(place):
        return ((column * 2 + place // POD) * POD + place % POD) * n_shard + here

    places = [lax.rem(me + ahead, RING) for ahead in (4, 3, 5, 2, 6, 1, 7, 0)]
    targets = [target(place) for place in places]

    def beside(pod):
        to = lax.rem(column + 2 * pod - 1 + columns, columns)
        return ((to * 2 + side) * POD + rep) * n_shard + here + 1

    def load(part):
        cols = pl.ds(part * 2 * wide, 2 * wide)
        return pltpu.make_async_copy(x_hbm.at[0, 0, :, cols], x.at[:, cols], x_sem.at[part])

    table_copy = pltpu.make_async_copy(table_hbm, table, table_sem)
    table_copy.start()
    for part in range(RING):
        load(part).start()

    barrier = pltpu.get_barrier_semaphore()

    def signal(device):
        pl.semaphore_signal(barrier, inc=1, device_id=device, device_id_type=LOGICAL)

    @pl.when(core == 1)
    def _():
        for device in targets[:-1]:
            signal(device)
            signal(device + 1)
        signal(targets[-1])
        for pod in range(2):
            signal(beside(pod))

    def share(half, step):
        return pltpu.make_async_remote_copy(
            src_ref=coeffs.at[half, places[step]], dst_ref=parts.at[half, core, side, rep],
            send_sem=rs_send, recv_sem=rs_recv.at[half, core, side],
            device_id=targets[step] + 1, device_id_type=LOGICAL)

    def swap(half, of_core, pod):
        return pltpu.make_async_remote_copy(
            src_ref=sums.at[half, of_core, pod], dst_ref=around.at[half, of_core, pod],
            send_sem=swap_send, recv_sem=swap_recv.at[half, of_core, pod],
            device_id=beside(pod), device_id_type=LOGICAL)

    def spread(half, to_core, pod, ahead):
        place = pod * POD + lax.rem(rep + ahead, POD)
        return pltpu.make_async_remote_copy(
            src_ref=mixed.at[half, to_core, pod], dst_ref=got.at[half, me],
            send_sem=ag_send, recv_sem=ag_recv.at[half],
            device_id=target(place) + to_core, device_id_type=LOGICAL)

    def bytes_of(blocks, sem):
        some = coeffs.at[0, pl.ds(0, blocks)]
        return pltpu.make_async_copy(some, some, sem)

    table_copy.wait()
    encode_operands(table, enc_cols, enc_rows)

    for half in range(2):
        for part in range(4):
            load(half * 4 + part).wait()
        groups = [x[:, pl.ds((half * RING + g) * wide, wide)] for g in range(RING)]
        out = encode(groups, enc_cols, enc_rows)
        for g in range(RING):
            coeffs[half, g] = out[:, g * 128:(g + 1) * 128]

        if half == 0:
            @pl.when(core == 0)
            def _():
                pl.semaphore_wait(barrier, RING)

            @pl.when(core == 1)
            def _():
                pl.semaphore_wait(barrier, RING + 1)

        for step in range(RING - 1):
            share(half, step).start()

        @pl.when(core == 0)
        def _():
            share(half, RING - 1).start()

        @pl.when(core == 1)
        def _():
            parts[half, 1, side, rep] = coeffs[half, me]

    def put_fresh(g, value):
        cols = pl.ds(g * wide, wide)
        fresh[0, 0, :, cols] = x[:, cols] - value

    decode_operands(table, dec_cols, dec_rows)
    decode([coeffs[half, g] for half in range(2) for g in range(RING)], dec_cols, dec_rows, put_fresh)

    @pl.when(core == 1)
    def _():
        for half in range(2):
            for of_core in (1, 0):
                for pod, own in ((side, 1), (1 - side, 0)):
                    bytes_of(POD - own * of_core, rs_recv.at[half, of_core, pod]).wait()
                    terms = [parts[half, of_core, pod, r] for r in range(POD)]
                    sums[half, of_core, pod] = (terms[0] + terms[1]) + (terms[2] + terms[3])
                    swap(half, of_core, pod).start()

        for half in range(2):
            for of_core in (1, 0):
                for pod in range(2):
                    swap(half, of_core, 1 - pod).wait_recv()
                    mixed[half, of_core, pod] = 0.5 * sums[half, of_core, pod] + 0.25 * (
                        sums[half, of_core, 1 - pod] + around[half, of_core, 1 - pod])
                    if of_core == 0:
                        spread(half, of_core, pod, 0).start()
                    else:
                        @pl.when(pod != side)
                        def _():
                            spread(half, of_core, pod, 0).start()

                        @pl.when(pod == side)
                        def _():
                            got[half, me] = mixed[half, of_core, pod]

                    for ahead in range(1, POD):
                        spread(half, of_core, pod, ahead).start()

        for half in range(2):
            bytes_of(RING - 1, rs_send).wait()
        bytes_of(RING, swap_send).wait()

    @pl.when(core == 0)
    def _():
        for half in range(2):
            bytes_of(RING, rs_send).wait()

    for half in range(2):
        @pl.when(core == 0)
        def _():
            bytes_of(RING, ag_recv.at[half]).wait()

        @pl.when(core == 1)
        def _():
            bytes_of(RING - 1, ag_recv.at[half]).wait()

        if half == 0:
            def put_update(g, value):
                update[:, pl.ds(g * wide, wide)] = value.astype(BF16)

            decode([got[0, g] for g in range(RING)], dec_cols, dec_rows, put_update)
        else:
            later[...] = got[1]

    @pl.when(core == 1)
    def _():
        for half in range(2):
            for to_core in range(2):
                bytes_of(RING - to_core, ag_send).wait()


def finish(fresh_in, update_in, later, dec_cols, dec_rows, fresh, update, second, sems):
    half = second.shape[1]
    copies = [
        pltpu.make_async_copy(fresh_in, fresh, sems.at[0]),
        pltpu.make_async_copy(update_in, update.at[0, :, pl.ds(0, half)], sems.at[1]),
    ]
    for copy in copies:
        copy.start()

    def put(g, value):
        second[:, pl.ds(g * GROUP * TILE, GROUP * TILE)] = value.astype(BF16)

    decode([later[g] for g in range(RING)], dec_cols, dec_rows, put)
    copies.append(pltpu.make_async_copy(second, update.at[0, :, pl.ds(half, half)], sems.at[2]))
    copies[-1].start()
    for copy in copies:
        copy.wait()


def local(momentum):
    rows, cols = momentum.shape[2:]
    table = jnp.asarray(tables())
    vmem = pl.BlockSpec(memory_space=pltpu.VMEM)
    anywhere = pl.BlockSpec(memory_space=pl.ANY)
    block = (KEEP, GROUP * KEEP)
    dma = pltpu.SemaphoreType.DMA
    fresh, *rest = pl.pallas_call(
        kernel,
        out_shape=(
            pltpu.VMEM(momentum.shape, F32),
            pltpu.VMEM((rows, cols // 2), BF16),
            pltpu.VMEM((RING, *block), F32),
            pltpu.VMEM((384, 512), BF16),
            pltpu.VMEM((64, 48), BF16),
        ),
        in_specs=[pl.BlockSpec(memory_space=pltpu.HBM)] * 2,
        out_specs=(vmem,) * 5,
        scratch_shapes=[
            pltpu.VMEM((rows, cols), F32),
            pltpu.VMEM(table.shape, F32),
            pltpu.VMEM((512, 256), BF16),
            pltpu.VMEM((16, 192), BF16),
            pltpu.VMEM((2, RING, *block), F32),
            pltpu.VMEM((2, 2, 2, POD, *block), F32),
            pltpu.VMEM((2, 2, 2, *block), F32),
            pltpu.VMEM((2, 2, 2, *block), F32),
            pltpu.VMEM((2, 2, 2, *block), F32),
            pltpu.VMEM((2, RING, *block), F32),
            dma((RING,)),
            dma,
            dma,
            dma((2, 2, 2)),
            dma,
            dma((2, 2, 2)),
            dma,
            dma((2,)),
        ],
        compiler_params=pltpu.CompilerParams(
            collective_id=0, has_side_effects=True, vmem_limit_bytes=60 * 1024 * 1024),
    )(momentum, table)
    return pl.pallas_call(
        finish,
        out_shape=(jax.ShapeDtypeStruct(fresh.shape, F32), jax.ShapeDtypeStruct((1, rows, cols), BF16)),
        in_specs=[anywhere] * 2 + [vmem] * 3,
        out_specs=(anywhere,) * 2,
        scratch_shapes=[pltpu.VMEM((rows, cols // 2), BF16), dma((3,))],
        compiler_params=pltpu.CompilerParams(vmem_limit_bytes=16 * 1024 * 1024),
    )(fresh, *rest)


def solution(mesh):
    in_specs = (P("outer", "rep", "shard", None),)
    out_specs = (P("outer", "rep", "shard", None), P("outer", "shard", None))
    return jax.shard_map(local, mesh=mesh, in_specs=in_specs, out_specs=out_specs, check_vma=False)
```

```python
import functools

import jax
import jax.numpy as jnp
import ml_dtypes
import numpy as np
from jax import lax
from jax.experimental import pallas as pl
from jax.experimental.pallas import tpu as pltpu
from jax.sharding import PartitionSpec as P

TILE = 64
KEEP = 16
RING = 8
POD = 4
GROUP = 8
LOGICAL = pl.DeviceIdType.LOGICAL
BF16 = jnp.bfloat16
F32 = jnp.float32


def low_basis():
    index = np.arange(TILE)
    freq = np.arange(KEEP)
    angles = np.pi * (2.0 * index[None, :] + 1.0) * freq[:, None] / (2.0 * TILE)
    scales = np.where(freq == 0, np.sqrt(1.0 / TILE), np.sqrt(2.0 / TILE))
    return (scales[:, None] * np.cos(angles)).astype(np.float32)


def halves(array):
    high = array.astype(ml_dtypes.bfloat16)
    low = (array - high.astype(np.float32)).astype(ml_dtypes.bfloat16)
    return high, low


def tables():
    basis = low_basis()
    high, low = (half.astype(np.float32) for half in halves(basis))
    out = np.zeros((208, 256), np.float32)
    out[:128, :128] = np.tile(basis, (GROUP, 2))
    out[:128, 128:] = np.tile(basis.T, (2, GROUP))
    out[128:144, :192] = np.concatenate([high, low, high], axis=1)
    out[144:, :48] = np.concatenate([high.T, high.T, low.T], axis=1)
    return out


def encode_operands(table, enc_cols, enc_rows):
    row = lax.broadcasted_iota(jnp.int32, (128, 128), 0)
    col = lax.broadcasted_iota(jnp.int32, (128, 128), 1)
    for place in range(4):
        lanes = pl.ds(place * 128, 128)
        high, low = split(jnp.where(col // KEEP == 2 * place + row // TILE, table[:128, 128:], 0.0))
        enc_cols[lanes, :128] = high
        enc_cols[lanes, 128:] = low
    enc_rows[...] = table[128:144, :192].astype(BF16)


def decode_operands(table, dec_cols, dec_rows):
    row = lax.broadcasted_iota(jnp.int32, (128, 128), 0)
    col = lax.broadcasted_iota(jnp.int32, (128, 128), 1)
    for place in range(4):
        lanes = pl.ds(place * 128, 128)
        high, low = split(jnp.where(row // KEEP == 2 * place + col // TILE, table[:128, :128], 0.0))
        dec_cols[:128, lanes] = high
        dec_cols[128:256, lanes] = high
        dec_cols[256:, lanes] = low
    dec_rows[...] = table[144:, :48].astype(BF16)


def split(value):
    high = value.astype(BF16)
    low = (value - high.astype(F32)).astype(BF16)
    return high, low


def dot(a, b):
    return jnp.dot(a, b, preferred_element_type=F32)


def encode(groups, enc_cols, enc_rows):
    high, low = split(jnp.concatenate(groups, axis=0))
    both = dot(high, enc_cols[...])
    right = both[:, :128] + both[:, 128:] + dot(low, enc_cols[:, :128])
    right = jnp.concatenate([right[g * TILE:(g + 1) * TILE] for g in range(len(groups))], axis=1)
    high, low = split(right)
    return dot(enc_rows[...], jnp.concatenate([high, high, low], axis=0))


def decode(blocks, dec_cols, dec_rows, put):
    high, low = split(jnp.concatenate(blocks, axis=0))
    right = dot(jnp.concatenate([high, low, high], axis=1), dec_cols[...])
    for g in range(len(blocks)):
        high, low = split(right[g * KEEP:(g + 1) * KEEP])
        put(g, dot(dec_rows[...], jnp.concatenate([high, low, high], axis=0)))


def kernel(x_hbm, table_hbm, fresh, later, dec_cols, dec_rows,
           x, table, enc_cols, enc_rows, coeffs, parts, sums, around, mixed, got,
           x_sem, table_sem, rs_send, rs_recv, swap_send, swap_recv, ag_send, ag_recv):
    outer, rep, shard = (lax.axis_index(axis) for axis in ("outer", "rep", "shard"))
    columns = lax.axis_size("outer") // 2
    column, side, core = outer // 2, outer % 2, shard % 2
    me = side * POD + rep
    wide = GROUP * TILE

    n_shard = lax.axis_size("shard")
    here = shard - core

    def target(place):
        return ((column * 2 + place // POD) * POD + place % POD) * n_shard + here

    places = [lax.rem(me + ahead, RING) for ahead in (4, 3, 5, 2, 6, 1, 7, 0)]
    targets = [target(place) for place in places]

    def beside(pod):
        to = lax.rem(column + 2 * pod - 1 + columns, columns)
        return ((to * 2 + side) * POD + rep) * n_shard + here + 1

    def load(part):
        cols = pl.ds(part * 2 * wide, 2 * wide)
        return pltpu.make_async_copy(x_hbm.at[0, 0, :, cols], x.at[:, cols], x_sem.at[part])

    table_copy = pltpu.make_async_copy(table_hbm, table, table_sem)
    table_copy.start()
    for part in range(RING):
        load(part).start()

    barrier = pltpu.get_barrier_semaphore()

    def signal(device):
        pl.semaphore_signal(barrier, inc=1, device_id=device, device_id_type=LOGICAL)

    @pl.when(core == 1)
    def _():
        for device in targets[:-1]:
            signal(device)
            signal(device + 1)
        signal(targets[-1])
        for pod in range(2):
            signal(beside(pod))

    def share(half, step):
        return pltpu.make_async_remote_copy(
            src_ref=coeffs.at[half, places[step]], dst_ref=parts.at[half, core, side, rep],
            send_sem=rs_send, recv_sem=rs_recv.at[half, core, side],
            device_id=targets[step] + 1, device_id_type=LOGICAL)

    def swap(half, of_core, pod):
        return pltpu.make_async_remote_copy(
            src_ref=sums.at[half, of_core, pod], dst_ref=around.at[half, of_core, pod],
            send_sem=swap_send, recv_sem=swap_recv.at[half, of_core, pod],
            device_id=beside(pod), device_id_type=LOGICAL)

    def spread(half, to_core, pod, ahead):
        place = pod * POD + lax.rem(rep + ahead, POD)
        return pltpu.make_async_remote_copy(
            src_ref=mixed.at[half, to_core, pod], dst_ref=got.at[half, me],
            send_sem=ag_send, recv_sem=ag_recv.at[half],
            device_id=target(place) + to_core, device_id_type=LOGICAL)

    def bytes_of(blocks, sem):
        some = coeffs.at[0, pl.ds(0, blocks)]
        return pltpu.make_async_copy(some, some, sem)

    table_copy.wait()
    encode_operands(table, enc_cols, enc_rows)

    for half in range(2):
        for part in range(4):
            load(half * 4 + part).wait()
        groups = [x[:, pl.ds((half * RING + g) * wide, wide)] for g in range(RING)]
        out = encode(groups, enc_cols, enc_rows)
        for g in range(RING):
            coeffs[half, g] = out[:, g * 128:(g + 1) * 128]

        if half == 0:
            @pl.when(core == 0)
            def _():
                pl.semaphore_wait(barrier, RING)

            @pl.when(core == 1)
            def _():
                pl.semaphore_wait(barrier, RING + 1)

        for step in range(RING - 1):
            share(half, step).start()

        @pl.when(core == 0)
        def _():
            share(half, RING - 1).start()

        @pl.when(core == 1)
        def _():
            parts[half, 1, side, rep] = coeffs[half, me]

    def put_fresh(g, value):
        cols = pl.ds(g * wide, wide)
        fresh[0, 0, :, cols] = x[:, cols] - value

    decode_operands(table, dec_cols, dec_rows)
    decode([coeffs[half, g] for half in range(2) for g in range(RING)], dec_cols, dec_rows, put_fresh)

    @pl.when(core == 1)
    def _():
        for half in range(2):
            for of_core in (1, 0):
                for pod, own in ((side, 1), (1 - side, 0)):
                    bytes_of(POD - own * of_core, rs_recv.at[half, of_core, pod]).wait()
                    terms = [parts[half, of_core, pod, r] for r in range(POD)]
                    sums[half, of_core, pod] = (terms[0] + terms[1]) + (terms[2] + terms[3])
                    swap(half, of_core, pod).start()

        for half in range(2):
            for of_core in (1, 0):
                for pod in range(2):
                    swap(half, of_core, 1 - pod).wait_recv()
                    mixed[half, of_core, pod] = 0.5 * sums[half, of_core, pod] + 0.25 * (
                        sums[half, of_core, 1 - pod] + around[half, of_core, 1 - pod])
                    if of_core == 0:
                        spread(half, of_core, pod, 0).start()
                    else:
                        @pl.when(pod != side)
                        def _():
                            spread(half, of_core, pod, 0).start()

                        @pl.when(pod == side)
                        def _():
                            got[half, me] = mixed[half, of_core, pod]

                    for ahead in range(1, POD):
                        spread(half, of_core, pod, ahead).start()

        for half in range(2):
            bytes_of(RING - 1, rs_send).wait()
        bytes_of(RING, swap_send).wait()

    @pl.when(core == 0)
    def _():
        for half in range(2):
            bytes_of(RING, rs_send).wait()

    for half in range(2):
        @pl.when(core == 0)
        def _():
            bytes_of(RING, ag_recv.at[half]).wait()

        @pl.when(core == 1)
        def _():
            bytes_of(RING - 1, ag_recv.at[half]).wait()

        later[half] = got[half]

    @pl.when(core == 1)
    def _():
        for half in range(2):
            for to_core in range(2):
                bytes_of(RING - to_core, ag_send).wait()


def finish(fresh_in, later, dec_cols, dec_rows, fresh, update, whole, sems):
    half = whole.shape[1] // 2
    wide = GROUP * TILE
    copies = [pltpu.make_async_copy(fresh_in, fresh, sems.at[0])]
    for part in range(2):
        cols = pl.ds(part * half, half)
        copies.append(pltpu.make_async_copy(whole.at[:, cols], update.at[0, :, cols], sems.at[1 + part]))
    copies[0].start()

    def put(g, value):
        whole[:, pl.ds(g * wide, wide)] = value.astype(BF16)
        if g % RING == RING - 1:
            copies[1 + g // RING].start()

    decode([later[part, g] for part in range(2) for g in range(RING)], dec_cols, dec_rows, put)
    for copy in copies:
        copy.wait()


def local(momentum):
    rows, cols = momentum.shape[2:]
    table = jnp.asarray(tables())
    vmem = pl.BlockSpec(memory_space=pltpu.VMEM)
    anywhere = pl.BlockSpec(memory_space=pl.ANY)
    block = (KEEP, GROUP * KEEP)
    dma = pltpu.SemaphoreType.DMA
    fresh, *rest = pl.pallas_call(
        kernel,
        out_shape=(
            pltpu.VMEM(momentum.shape, F32),
            pltpu.VMEM((2, RING, *block), F32),
            pltpu.VMEM((384, 512), BF16),
            pltpu.VMEM((64, 48), BF16),
        ),
        in_specs=[pl.BlockSpec(memory_space=pltpu.HBM)] * 2,
        out_specs=(vmem,) * 4,
        scratch_shapes=[
            pltpu.VMEM((rows, cols), F32),
            pltpu.VMEM(table.shape, F32),
            pltpu.VMEM((512, 256), BF16),
            pltpu.VMEM((16, 192), BF16),
            pltpu.VMEM((2, RING, *block), F32),
            pltpu.VMEM((2, 2, 2, POD, *block), F32),
            pltpu.VMEM((2, 2, 2, *block), F32),
            pltpu.VMEM((2, 2, 2, *block), F32),
            pltpu.VMEM((2, 2, 2, *block), F32),
            pltpu.VMEM((2, RING, *block), F32),
            dma((RING,)),
            dma,
            dma,
            dma((2, 2, 2)),
            dma,
            dma((2, 2, 2)),
            dma,
            dma((2,)),
        ],
        compiler_params=pltpu.CompilerParams(
            collective_id=0, has_side_effects=True, vmem_limit_bytes=60 * 1024 * 1024),
    )(momentum, table)
    return pl.pallas_call(
        finish,
        out_shape=(jax.ShapeDtypeStruct(fresh.shape, F32), jax.ShapeDtypeStruct((1, rows, cols), BF16)),
        in_specs=[anywhere] + [vmem] * 3,
        out_specs=(anywhere,) * 2,
        scratch_shapes=[pltpu.VMEM((rows, cols), BF16), dma((3,))],
        compiler_params=pltpu.CompilerParams(vmem_limit_bytes=16 * 1024 * 1024),
    )(fresh, *rest)


def solution(mesh):
    in_specs = (P("outer", "rep", "shard", None),)
    out_specs = (P("outer", "rep", "shard", None), P("outer", "shard", None))
    return jax.shard_map(local, mesh=mesh, in_specs=in_specs, out_specs=out_specs, check_vma=False)
```

```python
import functools

import jax
import jax.numpy as jnp
import ml_dtypes
import numpy as np
from jax import lax
from jax.experimental import pallas as pl
from jax.experimental.pallas import tpu as pltpu
from jax.sharding import PartitionSpec as P

TILE = 64
KEEP = 16
RING = 8
POD = 4
GROUP = 8
LOGICAL = pl.DeviceIdType.LOGICAL
BF16 = jnp.bfloat16
F32 = jnp.float32


def low_basis():
    index = np.arange(TILE)
    freq = np.arange(KEEP)
    angles = np.pi * (2.0 * index[None, :] + 1.0) * freq[:, None] / (2.0 * TILE)
    scales = np.where(freq == 0, np.sqrt(1.0 / TILE), np.sqrt(2.0 / TILE))
    return (scales[:, None] * np.cos(angles)).astype(np.float32)


def halves(array):
    high = array.astype(ml_dtypes.bfloat16)
    low = (array - high.astype(np.float32)).astype(ml_dtypes.bfloat16)
    return high, low


def tables():
    basis = low_basis()
    high, low = (half.astype(np.float32) for half in halves(basis))
    out = np.zeros((208, 256), np.float32)
    out[:128, :128] = np.tile(basis, (GROUP, 2))
    out[:128, 128:] = np.tile(basis.T, (2, GROUP))
    out[128:144, :192] = np.concatenate([high, low, high], axis=1)
    out[144:, :48] = np.concatenate([high.T, high.T, low.T], axis=1)
    return out


def encode_operands(table, enc_cols, enc_rows):
    row = lax.broadcasted_iota(jnp.int32, (128, 128), 0)
    col = lax.broadcasted_iota(jnp.int32, (128, 128), 1)
    for place in range(4):
        lanes = pl.ds(place * 128, 128)
        high, low = split(jnp.where(col // KEEP == 2 * place + row // TILE, table[:128, 128:], 0.0))
        enc_cols[lanes, :128] = high
        enc_cols[lanes, 128:] = low
    enc_rows[...] = table[128:144, :192].astype(BF16)


def decode_operands(table, dec_cols, dec_rows):
    row = lax.broadcasted_iota(jnp.int32, (128, 128), 0)
    col = lax.broadcasted_iota(jnp.int32, (128, 128), 1)
    for place in range(4):
        lanes = pl.ds(place * 128, 128)
        high, low = split(jnp.where(row // KEEP == 2 * place + col // TILE, table[:128, :128], 0.0))
        dec_cols[:128, lanes] = high
        dec_cols[128:256, lanes] = high
        dec_cols[256:, lanes] = low
    dec_rows[...] = table[144:, :48].astype(BF16)


def split(value):
    high = value.astype(BF16)
    low = (value - high.astype(F32)).astype(BF16)
    return high, low


def dot(a, b):
    return jnp.dot(a, b, preferred_element_type=F32)


def encode(groups, enc_cols, enc_rows):
    high, low = split(jnp.concatenate(groups, axis=0))
    both = dot(high, enc_cols[...])
    right = both[:, :128] + both[:, 128:] + dot(low, enc_cols[:, :128])
    right = jnp.concatenate([right[g * TILE:(g + 1) * TILE] for g in range(len(groups))], axis=1)
    high, low = split(right)
    return dot(enc_rows[...], jnp.concatenate([high, high, low], axis=0))


def decode(blocks, dec_cols, dec_rows, put):
    high, low = split(jnp.concatenate(blocks, axis=0))
    right = dot(jnp.concatenate([high, low, high], axis=1), dec_cols[...])
    for g in range(len(blocks)):
        high, low = split(right[g * KEEP:(g + 1) * KEEP])
        put(g, dot(dec_rows[...], jnp.concatenate([high, low, high], axis=0)))


def kernel(x_hbm, table_hbm, fresh, later, dec_cols, dec_rows,
           x, table, enc_cols, enc_rows, coeffs, parts, sums, around, mixed, got,
           x_sem, table_sem, rs_send, rs_recv, swap_send, swap_recv, ag_send, ag_recv):
    outer, rep, shard = (lax.axis_index(axis) for axis in ("outer", "rep", "shard"))
    columns = lax.axis_size("outer") // 2
    column, side, core = outer // 2, outer % 2, shard % 2
    me = side * POD + rep
    wide = GROUP * TILE

    n_shard = lax.axis_size("shard")
    here = shard - core

    def target(place):
        return ((column * 2 + place // POD) * POD + place % POD) * n_shard + here

    places = [lax.rem(me + ahead, RING) for ahead in (4, 3, 5, 2, 6, 1, 7, 0)]
    targets = [target(place) for place in places]

    def beside(pod):
        to = lax.rem(column + 2 * pod - 1 + columns, columns)
        return ((to * 2 + side) * POD + rep) * n_shard + here + 1

    def load(part):
        cols = pl.ds(part * 2 * wide, 2 * wide)
        return pltpu.make_async_copy(x_hbm.at[0, 0, :, cols], x.at[:, cols], x_sem.at[part])

    table_copy = pltpu.make_async_copy(table_hbm, table, table_sem)
    table_copy.start()
    for part in range(RING):
        load(part).start()

    barrier = pltpu.get_barrier_semaphore()

    def signal(device):
        pl.semaphore_signal(barrier, inc=1, device_id=device, device_id_type=LOGICAL)

    @pl.when(core == 1)
    def _():
        for device in targets[:-1]:
            signal(device)
            signal(device + 1)
        signal(targets[-1])
        for pod in range(2):
            signal(beside(pod))

    def share(half, step):
        return pltpu.make_async_remote_copy(
            src_ref=coeffs.at[half, places[step]], dst_ref=parts.at[half, core, side, rep],
            send_sem=rs_send, recv_sem=rs_recv.at[half, core, side],
            device_id=targets[step] + 1, device_id_type=LOGICAL)

    def swap(half, of_core, pod):
        return pltpu.make_async_remote_copy(
            src_ref=sums.at[half, of_core, pod], dst_ref=around.at[half, of_core, pod],
            send_sem=swap_send, recv_sem=swap_recv.at[half, of_core, pod],
            device_id=beside(pod), device_id_type=LOGICAL)

    def spread(half, to_core, pod, ahead):
        place = pod * POD + lax.rem(rep + ahead, POD)
        return pltpu.make_async_remote_copy(
            src_ref=mixed.at[half, to_core, pod], dst_ref=got.at[half, me],
            send_sem=ag_send, recv_sem=ag_recv.at[half],
            device_id=target(place) + to_core, device_id_type=LOGICAL)

    def bytes_of(blocks, sem):
        some = coeffs.at[0, pl.ds(0, blocks)]
        return pltpu.make_async_copy(some, some, sem)

    table_copy.wait()
    encode_operands(table, enc_cols, enc_rows)

    for half in range(2):
        for part in range(4):
            load(half * 4 + part).wait()
        groups = [x[:, pl.ds((half * RING + g) * wide, wide)] for g in range(RING)]
        out = encode(groups, enc_cols, enc_rows)
        for g in range(RING):
            coeffs[half, g] = out[:, g * 128:(g + 1) * 128]

        if half == 0:
            @pl.when(core == 0)
            def _():
                pl.semaphore_wait(barrier, RING)

            @pl.when(core == 1)
            def _():
                pl.semaphore_wait(barrier, RING + 1)

        for step in range(RING - 1):
            share(half, step).start()

        @pl.when(core == 0)
        def _():
            share(half, RING - 1).start()

        @pl.when(core == 1)
        def _():
            parts[half, 1, side, rep] = coeffs[half, me]

    def put_fresh(g, value):
        cols = pl.ds(g * wide, wide)
        fresh[0, 0, :, cols] = x[:, cols] - value

    decode_operands(table, dec_cols, dec_rows)
    decode([coeffs[half, g] for half in range(2) for g in range(RING)], dec_cols, dec_rows, put_fresh)

    @pl.when(core == 1)
    def _():
        for half in range(2):
            for of_core in (1, 0):
                for pod in (1, 0):
                    if of_core == 0:
                        bytes_of(POD, rs_recv.at[half, of_core, pod]).wait()
                    else:
                        @pl.when(pod == side)
                        def _():
                            bytes_of(POD - 1, rs_recv.at[half, of_core, pod]).wait()

                        @pl.when(pod != side)
                        def _():
                            bytes_of(POD, rs_recv.at[half, of_core, pod]).wait()

                    terms = [parts[half, of_core, pod, r] for r in range(POD)]
                    sums[half, of_core, pod] = (terms[0] + terms[1]) + (terms[2] + terms[3])
                    swap(half, of_core, pod).start()

        for half in range(2):
            for of_core in (1, 0):
                for pod in range(2):
                    swap(half, of_core, 1 - pod).wait_recv()
                    mixed[half, of_core, pod] = 0.5 * sums[half, of_core, pod] + 0.25 * (
                        sums[half, of_core, 1 - pod] + around[half, of_core, 1 - pod])
                    if of_core == 0:
                        spread(half, of_core, pod, 0).start()
                    else:
                        @pl.when(pod != side)
                        def _():
                            spread(half, of_core, pod, 0).start()

                        @pl.when(pod == side)
                        def _():
                            got[half, me] = mixed[half, of_core, pod]

                    for ahead in range(1, POD):
                        spread(half, of_core, pod, ahead).start()

        for half in range(2):
            bytes_of(RING - 1, rs_send).wait()
        bytes_of(RING, swap_send).wait()

    @pl.when(core == 0)
    def _():
        for half in range(2):
            bytes_of(RING, rs_send).wait()

    for half in range(2):
        @pl.when(core == 0)
        def _():
            bytes_of(RING, ag_recv.at[half]).wait()

        @pl.when(core == 1)
        def _():
            bytes_of(RING - 1, ag_recv.at[half]).wait()

        later[half] = got[half]

    @pl.when(core == 1)
    def _():
        for half in range(2):
            for to_core in range(2):
                bytes_of(RING - to_core, ag_send).wait()


def finish(fresh_in, later, dec_cols, dec_rows, fresh, update, whole, sems):
    half = whole.shape[1] // 2
    wide = GROUP * TILE
    copies = [pltpu.make_async_copy(fresh_in, fresh, sems.at[0])]
    for part in range(2):
        cols = pl.ds(part * half, half)
        copies.append(pltpu.make_async_copy(whole.at[:, cols], update.at[0, :, cols], sems.at[1 + part]))
    copies[0].start()

    def put(g, value):
        whole[:, pl.ds(g * wide, wide)] = value.astype(BF16)
        if g % RING == RING - 1:
            copies[1 + g // RING].start()

    decode([later[part, g] for part in range(2) for g in range(RING)], dec_cols, dec_rows, put)
    for copy in copies:
        copy.wait()


def local(momentum):
    rows, cols = momentum.shape[2:]
    table = jnp.asarray(tables())
    vmem = pl.BlockSpec(memory_space=pltpu.VMEM)
    anywhere = pl.BlockSpec(memory_space=pl.ANY)
    block = (KEEP, GROUP * KEEP)
    dma = pltpu.SemaphoreType.DMA
    fresh, *rest = pl.pallas_call(
        kernel,
        out_shape=(
            pltpu.VMEM(momentum.shape, F32),
            pltpu.VMEM((2, RING, *block), F32),
            pltpu.VMEM((384, 512), BF16),
            pltpu.VMEM((64, 48), BF16),
        ),
        in_specs=[pl.BlockSpec(memory_space=pltpu.HBM)] * 2,
        out_specs=(vmem,) * 4,
        scratch_shapes=[
            pltpu.VMEM((rows, cols), F32),
            pltpu.VMEM(table.shape, F32),
            pltpu.VMEM((512, 256), BF16),
            pltpu.VMEM((16, 192), BF16),
            pltpu.VMEM((2, RING, *block), F32),
            pltpu.VMEM((2, 2, 2, POD, *block), F32),
            pltpu.VMEM((2, 2, 2, *block), F32),
            pltpu.VMEM((2, 2, 2, *block), F32),
            pltpu.VMEM((2, 2, 2, *block), F32),
            pltpu.VMEM((2, RING, *block), F32),
            dma((RING,)),
            dma,
            dma,
            dma((2, 2, 2)),
            dma,
            dma((2, 2, 2)),
            dma,
            dma((2,)),
        ],
        compiler_params=pltpu.CompilerParams(
            collective_id=0, has_side_effects=True, vmem_limit_bytes=60 * 1024 * 1024),
    )(momentum, table)
    return pl.pallas_call(
        finish,
        out_shape=(jax.ShapeDtypeStruct(fresh.shape, F32), jax.ShapeDtypeStruct((1, rows, cols), BF16)),
        in_specs=[anywhere] + [vmem] * 3,
        out_specs=(anywhere,) * 2,
        scratch_shapes=[pltpu.VMEM((rows, cols), BF16), dma((3,))],
        compiler_params=pltpu.CompilerParams(vmem_limit_bytes=16 * 1024 * 1024),
    )(fresh, *rest)


def solution(mesh):
    in_specs = (P("outer", "rep", "shard", None),)
    out_specs = (P("outer", "rep", "shard", None), P("outer", "shard", None))
    return jax.shard_map(local, mesh=mesh, in_specs=in_specs, out_specs=out_specs, check_vma=False)
```
